256 devices in a mesh: dp: 4 (over y), frame: 64 (over x, z, core).
Axes of the slice: x: 4, y: 4, z: 8, core: 2. Of those that a mesh axis runs over, the one named last changes fastest.
Arguments:
- layer_in: bfloat16 [4, 16384, 2048], P('dp', 'frame'), may hold values from -6 to 6
- in_b: bfloat16 [4, 16384, 128], P('dp', 'frame'), may hold values from -0.5 to 0.5
- in_c: bfloat16 [4, 16384, 128], P('dp', 'frame'), may hold values from -0.5 to 0.5
- dt_raw: float32 [4, 32, 16384], P('dp', None, 'frame'), may hold values from -4 to 4
- a_log: float32 [32], replicated, may hold values from -16 to 1
- skip_gain: float32 [32], replicated, may hold values from 0.5 to 1.5
- dt_bias: float32 [32], replicated, may hold values from -0.5 to 0.5
- foot_map: float32 [12, 2048], replicated, may hold values from -0.125 to 0.125
- contact: int32 [4, 16384], P('dp', 'frame'), may hold values 0 or 1
- out_grad: bfloat16 [4, 16384, 2048], P('dp', 'frame'), may hold values from -27 to 27
Outputs:
- grad_in: bfloat16 [4, 16384, 2048], P('dp', 'frame')
- grad_b: float32 [4, 16384, 128], P('dp', 'frame')
- grad_c: float32 [4, 16384, 128], P('dp', 'frame')
- grad_dt: float32 [4, 32, 16384], P('dp', None, 'frame')
- head_grads: float32 [3, 32], replicated
The draws below stay inside these ranges and needn't reach their ends.
All inputs are finite; a program needn't handle non-finite values. No bound on the sum of `contact` on one device may be relied on, other than what follows from the above.
Results may differ from the reference program's by a relative error of at most 0.0013.
Values sent between devices are 32-bit elements; how exact they have to be, the bound alone decides.
A program may use at most 320 MiB of HBM per device.

```python
import math
import jax
import jax.numpy as jnp
from jax import lax

H = 32
P_SIZE = 64
N = 128
GROUP = 128
FEET = 12
FR_DEV = 256
HP = 2048
FRAMES = 16384
SESSIONS = 4


def draw_a_log(key, part):
    order_key = jax.random.fold_in(key, 11)
    rate_key = jax.random.fold_in(key, 12)
    ranks = jax.random.permutation(order_key, H)
    slow = ranks >= H // 2
    level = jax.random.uniform(rate_key, (H,), jnp.float32)
    slow_rate = jnp.exp(math.log(0.2) + level * math.log(5.0)) / FRAMES
    fast_rate = jnp.exp(math.log(3.0) + level * math.log(8.0 / 3.0)) / GROUP
    rate = jnp.where(slow, slow_rate, fast_rate)
    return jnp.log(rate / 0.7)


def draw_dt_raw(key, part):
    noise_key = jax.random.fold_in(key, 21)
    block_key = jax.random.fold_in(key, 22)
    blocks = FRAMES // FR_DEV
    noise = 0.5 * jax.random.normal(noise_key, (SESSIONS, H, FRAMES), jnp.float32)
    offset = jax.random.uniform(block_key, (SESSIONS, H, blocks), jnp.float32, -0.7, 0.7)
    value = noise + jnp.repeat(offset, FR_DEV, axis=2)
    return jnp.clip(value, -4.0, 4.0)


def draw_out_grad(key, part):
    base_key = jax.random.fold_in(key, 31)
    column_key = jax.random.fold_in(key, 32)
    position = jnp.arange(FRAMES, dtype=jnp.float32) / FRAMES
    column = jnp.exp(jax.random.uniform(column_key, (HP,), jnp.float32, math.log(0.3), math.log(3.0)))
    base = jnp.clip(jax.random.normal(base_key, (SESSIONS, FRAMES, HP), jnp.float32), -4.0, 4.0)
    rise = 0.6 + 1.2 * position
    return (base * rise[None, :, None] * column[None, None, :]).astype(jnp.bfloat16)


def plant(result, rng, least, largest):
    shape = result.shape
    spot = [jax.random.randint(jax.random.fold_in(rng, axis), (), 0, shape[axis]) for axis in range(len(shape))]
    result = result.at[tuple(spot)].set(least)
    longest = shape.index(max(shape))
    spot[longest] = (spot[longest] + 1) % shape[longest]
    return result.at[tuple(spot)].set(largest)


def level_of(key, shape, cuts, smallest, top_value):
    level = 1.0
    for dim, shards_of in cuts:
        heights = jax.random.uniform(jax.random.fold_in(jax.random.fold_in(key, 6), dim), (shards_of,), jnp.float32, smallest / len(cuts), top_value / len(cuts))
        level = level * jnp.repeat(jnp.exp(heights), shape[dim] // shards_of).reshape((-1,) + (1,) * (len(shape) - 1 - dim))
    return level


def gaussian(key, shape, scale, reach, cuts=(), held_as=jnp.bfloat16):
    values = scale * jax.random.normal(key, shape, jnp.float32)
    if cuts:
        values = values * level_of(key, shape, cuts, -0.22, 0.18)
    return jnp.clip(values, -reach, reach).astype(held_as)


def setup_inputs(seed: int = 0) -> dict:
    streams_of = jax.random.split(jax.random.key(seed), 11)
    return {
        "layer_in": gaussian(streams_of[0], (SESSIONS, FRAMES, HP), 1.0, 6.0, ((0, 4), (1, 64))),
        "in_b": gaussian(streams_of[1], (SESSIONS, FRAMES, N), N ** -0.5, 0.5, ((0, 4), (1, 64))),
        "in_c": gaussian(streams_of[2], (SESSIONS, FRAMES, N), N ** -0.5, 0.5, ((0, 4), (1, 64))),
        "dt_raw": draw_dt_raw(jax.random.fold_in(streams_of[10], 71), 0),
        "a_log": draw_a_log(jax.random.fold_in(streams_of[10], 71), 0),
        "skip_gain": jnp.clip(jax.random.uniform(streams_of[5], (H,), jnp.float32, 0.5, 1.5), 0.5, 1.5),
        "dt_bias": jnp.clip(jax.random.uniform(streams_of[6], (H,), jnp.float32, -0.5, 0.5), -0.5, 0.5),
        "foot_map": gaussian(streams_of[7], (FEET, HP), HP ** -0.5, 0.125, (), jnp.float32),
        "contact": plant((jax.random.randint(streams_of[8], (SESSIONS, FRAMES), 0, 2) < 1).astype(jnp.int32), jax.random.fold_in(streams_of[8], 1), 0, 1),
        "out_grad": draw_out_grad(jax.random.fold_in(streams_of[10], 71), 0),
    }


HIGH = lax.Precision.HIGHEST

def group_pass(state, pieces, decay_rate, skip_gain):
    block_x, block_b, block_c, block_step = pieces
    width = block_step.shape[1]
    row_ids = lax.broadcasted_iota(jnp.int32, (width, width), 0)
    col_ids = lax.broadcasted_iota(jnp.int32, (width, width), 1)
    upper = (row_ids <= col_ids).astype(jnp.float32)
    logdec = block_step * decay_rate[:, None]
    cumul = jnp.dot(logdec, upper, precision=HIGH)
    causal = (row_ids >= col_ids)[None]
    spread = cumul[:, :, None] - cumul[:, None, :]
    within = jnp.where(causal, jnp.exp(jnp.where(causal, spread, 0.0)), 0.0)
    scores = jnp.dot(block_c, block_b.T, precision=HIGH)
    mixing = scores[None] * within * block_step[:, None, :]
    inner = jnp.einsum('hts,shp->thp', mixing, block_x, precision=HIGH)
    carried = jnp.einsum('tn,hpn->thp', block_c, state, precision=HIGH) * jnp.exp(cumul).T[:, :, None]
    output = inner + carried + skip_gain[None, :, None] * block_x
    tail_weight = jnp.exp(cumul[:, -1:] - cumul) * block_step
    weighted = block_x * tail_weight.T[:, :, None]
    fresh = jnp.einsum('shp,sn->hpn', weighted, block_b, precision=HIGH)
    new_state = jnp.exp(cumul[:, -1])[:, None, None] * state + fresh
    return (new_state, output)

def run_blocks(layer_x, layer_b, layer_c, raw_step, a_log, skip_gain, dt_bias, state):
    length = layer_x.shape[0]
    count = length // GROUP
    step = jax.nn.softplus(raw_step + dt_bias[:, None])
    decay_rate = -jnp.exp(a_log)
    block_x = layer_x.reshape(count, GROUP, H, P_SIZE)
    block_b = layer_b.reshape(count, GROUP, N)
    block_c = layer_c.reshape(count, GROUP, N)
    block_step = step.reshape(H, count, GROUP).transpose(1, 0, 2)

    def advance(carry, pieces):
        return group_pass(carry, pieces, decay_rate, skip_gain)
    final, outputs = lax.scan(jax.checkpoint(advance), state, (block_x, block_b, block_c, block_step))
    return (outputs.reshape(length, H * P_SIZE), final)

def foot_cotangent(output, contact, foot_map):
    velocity = jnp.einsum('kc,tc->kt', foot_map, output, precision=HIGH)
    touch = contact.astype(jnp.float32)[None, :]
    before = jnp.pad(velocity[:, :-1], ((0, 0), (1, 0)))
    started = (lax.broadcasted_iota(jnp.int32, (1, velocity.shape[1]), 1) > 0).astype(jnp.float32)
    slide = touch * started * (velocity - before)
    after = jnp.pad(slide[:, 1:], ((0, 0), (0, 1)))
    return jnp.einsum('kt,kc->tc', slide - after, foot_map, precision=HIGH)

def reference(layer_in, in_b, in_c, dt_raw, a_log, skip_gain, dt_bias, foot_map, contact, out_grad):

    def session(pieces):
        session_x, session_b, session_c, session_step, session_touch, session_given = pieces

        def forward(part_x, part_b, part_c, part_step, part_log, part_skip, part_bias):
            start = jnp.zeros((H, P_SIZE, N), jnp.float32)
            return run_blocks(part_x, part_b, part_c, part_step, part_log, part_skip, part_bias, start)[0]
        output, pull = jax.vjp(forward, session_x.astype(jnp.float32), session_b.astype(jnp.float32), session_c.astype(jnp.float32), session_step, a_log, skip_gain, dt_bias)
        cotangent = session_given.astype(jnp.float32) + foot_cotangent(output, session_touch, foot_map)
        grads = pull(cotangent)
        return (grads[0].astype(jnp.bfloat16), grads[1], grads[2], grads[3], jnp.stack([grads[4], grads[5], grads[6]]))
    grad_x, grad_b, grad_c, grad_step, per_session = lax.map(session, (layer_in, in_b, in_c, dt_raw, contact, out_grad))
    return (grad_x, grad_b, grad_c, grad_step, lax.optimization_barrier(jnp.sum(per_session, axis=0)))
```

```python
import functools

import jax
import jax.numpy as jnp
from jax import lax
from jax.experimental import pallas as pl
from jax.experimental.pallas import tpu as pltpu
from jax.sharding import PartitionSpec as P

MESH = pl.DeviceIdType.MESH
HIGH = lax.Precision.HIGHEST
F32, BF16 = jnp.float32, jnp.bfloat16
H, PS, N, T, HP, FEET = 32, 64, 128, 256, 2048, 12
PAIRS = HP // 128
LOG2E = 1.4426950408889634
KL = 512
G1 = 16


def nn(a, b):
    return lax.dot_general(a, b, (((1,), (0,)), ((), ())), preferred_element_type=F32)


def nt(a, b):
    return lax.dot_general(a, b, (((1,), (1,)), ((), ())), preferred_element_type=F32)


def nn_hi(a, b):
    return lax.dot_general(
        a, b, (((1,), (0,)), ((), ())), precision=HIGH, preferred_element_type=F32
    )


def nt_hi(a, b):
    return lax.dot_general(
        a, b, (((1,), (1,)), ((), ())), precision=HIGH, preferred_element_type=F32
    )


def split(v):
    hi = v.astype(BF16)
    return hi, (v - hi.astype(F32)).astype(BF16)


def split3(v):
    hi = v.astype(BF16)
    rest = v - hi.astype(F32)
    mid = rest.astype(BF16)
    return hi, mid, (rest - mid.astype(F32)).astype(BF16)


def iota(shape, dim):
    return lax.broadcasted_iota(jnp.int32, shape, dim)


def kernel(
    dp_n,
    nf,
    x_ref,
    b_ref,
    c_ref,
    dt_ref,
    al_ref,
    sk_ref,
    bi_ref,
    f_ref,
    ct_ref,
    og_ref,
    gx_ref,
    gb_ref,
    gc_ref,
    gdt_ref,
    hg_ref,
    local_f,
    local_r,
    sib_f,
    sib_r,
    half_f,
    half_r,
    got_f,
    got_r,
    ret_f,
    ret_r,
    s_in,
    g_end,
    cexp,
    sexp,
    yv,
    dz,
    zhi,
    zlo,
    dyhi,
    dylo,
    fpad,
    c2_ref,
    ld_ref,
    sg_ref,
    sc_ref,
    sct_ref,
    ds0,
    ds1,
    dec_mine,
    decs,
    sib_dec,
    dec_all,
    vel,
    vel_prev,
    vel_next,
    gd_local,
    gd_got,
    gd_ret,
    gd_end,
    p1,
    p2,
    row_d,
    row_b,
    hsum,
    hgot1,
    hmid,
    hgot2,
    ssem,
    rsem,
):
    chips = nf // 2
    me_dp = lax.axis_index("dp")
    me = lax.axis_index("frame")
    chip, core = me // 2, me % 2
    sib = me + 1 - 2 * core
    first = core == 0
    lbs = chips // 8
    lanes = HP // lbs
    g2n = dp_n * (nf // G1)

    def ring(k, base=None):
        return lax.rem(me + k, nf)

    barrier = pltpu.get_barrier_semaphore()

    @pl.loop(1, nf)
    def _(k):
        pl.semaphore_signal(barrier, inc=1, device_id=(me_dp, ring(k)), device_id_type=MESH)

    group = me // G1
    low = me % G1

    @pl.loop(1, dp_n)
    def _(k):
        d = lax.rem(me_dp + k, dp_n)

        @pl.loop(0, nf // G1)
        def _(j):
            pl.semaphore_signal(
                barrier, inc=1, device_id=(d, j * G1 + low), device_id_type=MESH
            )

    def remote(src, dst, s, r, dev, dp=None):
        return pltpu.make_async_remote_copy(
            src_ref=src,
            dst_ref=dst,
            send_sem=ssem.at[s],
            recv_sem=rsem.at[r],
            device_id=(me_dp if dp is None else dp, dev),
            device_id_type=MESH,
        )

    eye = (iota((T, T), 0) == iota((T, T), 1)).astype(F32)
    rows8 = iota((8, H), 0)
    rows = jnp.where(
        rows8 == 0, al_ref[...], jnp.where(rows8 == 1, sk_ref[...], bi_ref[...])
    )
    eye32 = (iota((H, H), 0) == iota((H, H), 1)).astype(F32)
    cols = nt_hi(eye32, rows)
    rate = -jnp.exp(cols[:, 0:1])
    raw = dt_ref[...] + cols[:, 2:3]
    tail = jnp.exp(-jnp.abs(raw))
    step = jnp.maximum(raw, 0.0) + jnp.log1p(tail)
    sg_ref[...] = jnp.where(raw >= 0, 1.0, tail) / (1.0 + tail)
    ld = rate * step
    ld_ref[...] = ld
    upper = (iota((T, T), 0) <= iota((T, T), 1)).astype(F32)
    c2 = nn_hi(ld, upper) * LOG2E
    for i in range(PAIRS):
        c2_ref[i, 0:2, :] = c2[2 * i : 2 * i + 2]
    c3 = jnp.concatenate(split3(nt_hi(eye, c2)), axis=1)
    s3 = jnp.concatenate(split3(nt_hi(eye, step)), axis=1)
    spread_k = (iota((96, KL), 0) % H == iota((96, KL), 1) % H).astype(BF16)
    c_feet = nn(c3, spread_k)
    dec_mine[...] = jnp.broadcast_to(c_feet[T - 1 : T, 0:128], (8, 128))
    eye_b = (iota((N, N), 0) == iota((N, N), 1)).astype(BF16)
    bb, cc = b_ref[...], c_ref[...]
    bt = nt(eye_b, bb).astype(BF16)
    ct = nt(eye_b, cc).astype(BF16)

    fpad[...] = jnp.zeros_like(fpad)
    fpad[0:FEET, :] = f_ref[...]

    @pl.loop(0, PAIRS)
    def _(i):
        blk = pl.ds(pl.multiple_of(i * 128, 128), 128)
        e3 = (iota((96, 128), 0) % H == 2 * i + iota((96, 128), 1) // PS).astype(BF16)
        cb, sb = nn(c3, e3), nn(s3, e3)
        cexp[:, blk] = cb
        sexp[:, blk] = sb
        z = sb * x_ref[:, blk].astype(F32)
        hi, lo = split(z)
        zhi[:, blk] = hi
        zlo[:, blk] = lo
        hi, lo = split(jnp.exp2(cb[T - 1 : T] - cb) * z)
        local_f[:, blk] = nn(bt, hi) + nn(bt, lo)
        hi, lo = split(jnp.exp2(cb) * og_ref[:, blk].astype(F32))
        local_r[:, blk] = nn(ct, hi) + nn(ct, lo)

    pl.semaphore_wait(barrier, nf - 1 + (dp_n - 1) * (nf // G1))

    mine_half = pl.ds(pl.multiple_of(core * 64, 64), 64)
    sib_half = pl.ds(pl.multiple_of(64 - core * 64, 64), 64)
    ex_dec = remote(dec_mine, sib_dec, 5, 5, sib)
    ex = [
        remote(local_f.at[sib_half], sib_f.at[sib_half], 1, 1, sib),
        remote(local_r.at[sib_half], sib_r.at[sib_half], 2, 2, sib),
        remote(local_f.at[mine_half], sib_f.at[mine_half], 3, 3, sib),
        remote(local_r.at[mine_half], sib_r.at[mine_half], 4, 4, sib),
    ]
    ex_dec.start()
    ex[0].start()
    ex[1].start()

    @pl.loop(1, nf)
    def _(k):
        remote(dec_mine, decs.at[me], 0, 0, ring(k)).start()

    decs[me] = dec_mine[...]

    scores = nt(cc, bb)
    sc_ref[...] = jnp.where(iota((T, T), 0) >= iota((T, T), 1), scores, 0.0)
    scores = nt(bb, cc)
    sct_ref[...] = jnp.where(iota((T, T), 0) <= iota((T, T), 1), scores, 0.0)

    def sib_decay(i):
        e1 = (iota((128, 128), 0) == 2 * i + iota((128, 128), 1) // PS).astype(F32)
        return jnp.exp2(nn_hi(sib_dec[...], e1))[0:1]

    ex_dec.wait()
    ex[0].wait()
    ex[1].wait()

    @pl.loop(0, PAIRS)
    def _(i):
        blk = pl.ds(pl.multiple_of(i * 128, 128), 128)
        d_sib = sib_decay(i)
        d_me = jnp.exp2(cexp[pl.ds(T - 8, 8), blk])[7:8]
        one = jnp.ones_like(d_me)
        half_f[:, blk] = (
            jnp.where(first, d_sib, one) * local_f[mine_half, blk]
            + jnp.where(first, one, d_me) * sib_f[mine_half, blk]
        )
        half_r[:, blk] = (
            jnp.where(first, one, d_sib) * local_r[mine_half, blk]
            + jnp.where(first, d_me, one) * sib_r[mine_half, blk]
        )

    def part(o):
        return (
            pl.ds(pl.multiple_of(o // lbs * 8, 8), 8),
            pl.ds(pl.multiple_of(o % lbs * lanes, 128), lanes),
        )

    @pl.loop(1, chips)
    def _(k):
        o = lax.rem(chip + k, chips)
        r, l = part(o)
        remote(half_f.at[r, l], got_f.at[chip], 6, 6, o * 2 + core).start()
        remote(half_r.at[r, l], got_r.at[chip], 7, 7, o * 2 + core).start()

    ex[2].start()
    ex[3].start()
    my_r, my_l = part(chip)
    got_f[chip] = half_f[my_r, my_l]
    got_r[chip] = half_r[my_r, my_l]

    low_lanes = iota((128, 128), 1) < PS

    def inner(i):
        blk = pl.ds(pl.multiple_of(i * 128, 128), 128)
        rhs = jnp.concatenate([zhi[:, blk], zlo[:, blk]], axis=1)
        cb = cexp[:, blk]
        for r in range(2):
            seen = 128 * (r + 1)
            at = slice(128 * r, seen)
            outs = []
            for e in range(2):
                col = cb[at, PS * e : PS * e + 1]
                row = c2_ref[i, e : e + 1, 0:seen]
                mix = sc_ref[at, 0:seen] * jnp.exp2(jnp.minimum(col - row, 0.0))
                hi, lo = split(mix)
                res = nn(hi, rhs[0:seen]) + nn(lo, rhs[0:seen])
                outs.append(res[:, 0:128] + res[:, 128:256])
            yv[at, blk] = jnp.where(low_lanes, outs[0], outs[1])

    pl.loop(0, PAIRS // 2)(inner)

    def arrived(buf, n, s):
        view = buf.at[pl.ds(0, n)]
        d = remote(view, view, s, s, sib)
        d.wait()

    arrived(decs, nf - 1, 0)
    dall = decs[:, 0, :]
    dec_all[...] = jnp.exp2(dall)
    pairsum = (iota((chips, nf), 0) == iota((chips, nf), 1) // 2).astype(F32)
    chip_log = nn_hi(pairsum, dall)
    head0 = chip % lbs * (lanes // PS)
    spread_l = (iota((128, lanes), 0) == head0 + iota((128, lanes), 1) // PS).astype(F32)
    chip_dec = jnp.exp2(nn_hi(chip_log, spread_l))

    arrived(got_f, chips - 1, 6)
    acc = jnp.zeros((8, lanes), F32)
    for q in range(chips):
        ret_f[q] = acc
        acc = got_f[q] + chip_dec[q : q + 1] * acc

    @pl.loop(1, chips)
    def _(k):
        o = lax.rem(chip + k, chips)
        r = pl.ds(pl.multiple_of(core * 64 + chip // lbs * 8, 8), 8)
        remote(ret_f.at[o], s_in.at[r, my_l], 8, 8, o * 2 + core).start()

    arrived(got_r, chips - 1, 7)
    acc = jnp.zeros((8, lanes), F32)
    for q in reversed(range(chips)):
        ret_r[q] = acc
        acc = got_r[q] + chip_dec[q : q + 1] * acc

    @pl.loop(1, chips)
    def _(k):
        o = lax.rem(chip + k, chips)
        r = pl.ds(pl.multiple_of(core * 64 + chip // lbs * 8, 8), 8)
        remote(ret_r.at[o], g_end.at[r, my_l], 9, 9, o * 2 + core).start()

    own = pl.ds(pl.multiple_of(core * 64 + chip // lbs * 8, 8), 8)
    s_in[own, my_l] = ret_f[chip]
    g_end[own, my_l] = ret_r[chip]

    pl.loop(PAIRS // 2, PAIRS)(inner)

    arrived(ret_f, chips - 1, 8)
    back_f = remote(s_in.at[mine_half], s_in.at[mine_half], 10, 10, sib)
    back_f.start()
    ex[2].wait()
    ex[3].wait()
    back_f.wait()

    vel[...] = jnp.zeros_like(vel)
    sk8 = jnp.broadcast_to(sk_ref[...], (8, H))

    @pl.loop(0, PAIRS)
    def _(i):
        blk = pl.ds(pl.multiple_of(i * 128, 128), 128)
        d_sib = sib_decay(i)
        state = s_in[:, blk]
        state = jnp.where(first, state, sib_f[:, blk] + d_sib * state)
        s_in[:, blk] = state
        hi, lo = split(state)
        y = yv[:, blk] + jnp.exp2(cexp[:, blk]) * (nn(cc, hi) + nn(cc, lo))
        yv[:, blk] = y
        e1 = (iota((H, 128), 0) == 2 * i + iota((H, 128), 1) // PS).astype(F32)
        out = y + nn_hi(sk8, e1)[0:1] * x_ref[:, blk].astype(F32)
        hi, lo = split(out)
        fhi, flo = split(fpad[:, blk])
        vel[...] += nt(hi, fhi) + nt(lo, fhi) + nt(hi, flo)

    touch = jnp.broadcast_to(ct_ref[...].astype(F32), (8, T))
    touch = nt_hi(eye, touch)[:, 0:1]
    lane = iota((T, 128), 1)
    row = iota((T, 128), 0)
    v = jnp.where(lane == FEET, touch, vel[...])
    vel[...] = v
    to_next = remote(vel.at[pl.ds(T - 8, 8)], vel_prev, 12, 12, ring(1))
    to_prev = remote(vel.at[pl.ds(0, 8)], vel_next, 13, 13, ring(nf - 1))
    to_next.start()
    to_prev.start()
    to_next.wait()
    to_prev.wait()
    feet = lane < FEET
    before = jnp.where(row == 0, vel_prev[7:8, :], pltpu.roll(v, 1, 0))
    slide = jnp.where(
        feet & ((row > 0) | (me > 0)), touch * (v - before), 0.0
    )
    nxt = vel_next[0:1, :]
    edge = nxt[:, FEET : FEET + 1] * (nxt - v[T - 1 : T, :])
    edge = jnp.where((iota((1, 128), 1) < FEET) & (me < nf - 1), edge, 0.0)
    change = slide - jnp.where(row == T - 1, edge, pltpu.roll(slide, T - 1, 0))
    chi, clo = split(change)

    feet_of = (iota((128, KL), 0) == iota((128, KL), 1) // H).astype(BF16)
    hi, lo = split(jnp.exp2(c_feet) * (nn(chi, feet_of) + nn(clo, feet_of)))
    gd_local[...] = nn(ct, hi) + nn(ct, lo)

    def tile(o):
        return (
            pl.ds(pl.multiple_of(o // 4 * 8, 8), 8),
            pl.ds(pl.multiple_of(o % 4 * 128, 128), 128),
        )

    @pl.loop(1, nf)
    def _(k):
        o = ring(k)
        r, l = tile(o)
        remote(gd_local.at[r, l], gd_got.at[me], 14, 14, o).start()

    my_tr, my_tl = tile(me)
    gd_got[me] = gd_local[my_tr, my_tl]

    arrived(ret_r, chips - 1, 9)
    back_r = remote(g_end.at[mine_half], g_end.at[mine_half], 11, 11, sib)
    back_r.start()

    @pl.loop(0, PAIRS)
    def _(i):
        blk = pl.ds(pl.multiple_of(i * 128, 128), 128)
        fhi, flo = split(fpad[:, blk])
        dy = og_ref[:, blk].astype(F32) + nn(chi, fhi) + nn(clo, fhi) + nn(chi, flo)
        hi, lo = split(dy)
        dyhi[:, blk] = hi
        dylo[:, blk] = lo

    ds0[...] = jnp.zeros_like(ds0)
    ds1[...] = jnp.zeros_like(ds1)
    zero_b = jnp.zeros((128, 128), BF16)

    def backward(i):
        blk = pl.ds(pl.multiple_of(i * 128, 128), 128)
        dh, dl = dyhi[:, blk], dylo[:, blk]
        rhs = jnp.concatenate([dh, dl], axis=1)
        twice = jnp.concatenate([dh, dh], axis=1)
        cb = cexp[:, blk]
        for r, acc in ((0, ds0), (1, ds1)):
            at, on = slice(128 * r, 128 * r + 128), slice(128 * r, T)
            zh, zl = zhi[at, blk], zlo[at, blk]
            outs = []
            total = acc[...]
            for e in range(2):
                keep = low_lanes if e == 0 else ~low_lanes
                zhe = jnp.where(keep, zh, zero_b)
                zle = jnp.where(keep, zl, zero_b)
                col = cb[at, PS * e : PS * e + 1]
                fall = jnp.exp2(jnp.minimum(c2_ref[i, e : e + 1, on] - col, 0.0))
                w = nt(jnp.concatenate([zhe, zle], axis=1), twice[on]) + nt(zhe, dl[on])
                total = total + fall * w
                hi, lo = split(sct_ref[at, on] * fall)
                res = nn(hi, rhs[on]) + nn(lo, rhs[on])
                outs.append(res[:, 0:128] + res[:, 128:256])
            acc[...] = total
            dz[at, blk] = jnp.where(low_lanes, outs[0], outs[1])

    pl.loop(0, PAIRS // 2)(backward)

    arrived(gd_got, nf - 1, 14)
    acc = jnp.zeros((8, 128), F32)
    for q in reversed(range(nf)):
        gd_ret[q] = acc
        acc = gd_got[q] + dec_all[q : q + 1] * acc

    @pl.loop(1, nf)
    def _(k):
        o = ring(k)
        remote(gd_ret.at[o], gd_end.at[my_tr, my_tl], 15, 15, o).start()

    gd_end[my_tr, my_tl] = gd_ret[me]

    pl.loop(PAIRS // 2, PAIRS)(backward)

    m0 = iota((128, T), 0) <= iota((128, T), 1)
    m1 = iota((128, 128), 0) <= iota((128, 128), 1)
    dst = jnp.concatenate(
        [
            jnp.where(m0, ds0[...], 0.0),
            jnp.concatenate(
                [jnp.zeros((128, 128), F32), jnp.where(m1, ds1[...], 0.0)], axis=1
            ),
        ],
        axis=0,
    )
    hi, lo = split(dst)
    gb_ref[...] = nn(hi, cc) + nn(lo, cc)
    eye_t = eye.astype(BF16)
    hi = nt(eye_t, hi).astype(BF16)
    lo = nt(eye_t, lo).astype(BF16)
    gc_ref[...] = nn(hi, bb) + nn(lo, bb)

    @pl.loop(0, PAIRS)
    def _(i):
        blk = pl.ds(pl.multiple_of(i * 128, 128), 128)
        dy = dyhi[:, blk].astype(F32) + dylo[:, blk].astype(F32)
        hi, lo = split(jnp.exp2(cexp[:, blk]) * dy)
        shi, slo = split(s_in[:, blk])
        gc_ref[...] += nt(hi, shi) + nt(lo, shi) + nt(hi, slo)

    back_r.wait()
    view = gd_ret.at[pl.ds(0, nf - 1)]
    remote(view, view, 15, 15, sib).wait()

    p1[...] = jnp.zeros_like(p1)
    p2[...] = jnp.zeros_like(p2)
    gdh, gdl = split(gd_end[:, 0 : FEET * H])

    @pl.loop(0, PAIRS)
    def _(i):
        blk = pl.ds(pl.multiple_of(i * 128, 128), 128)
        here = iota((H, 128), 0) == 2 * i + iota((H, 128), 1) // PS
        e1 = here.astype(F32)
        e1b = here.astype(BF16)
        ff = fpad[0:16, blk]
        big = jnp.concatenate([ff[k : k + 1] * e1 for k in range(FEET)], axis=0)
        bhi, blo = split(big)
        grad = g_end[:, blk]
        grad = jnp.where(first, sib_r[:, blk] + sib_decay(i) * grad, grad)
        grad = grad + nn(gdh, bhi) + nn(gdl, bhi) + nn(gdh, blo)
        ghi, glo = split(grad)
        cb, sb = cexp[:, blk], sexp[:, blk]
        last = cb[T - 1 : T]
        fade = jnp.exp2(last - cb)
        x = x_ref[:, blk].astype(F32)
        dzb = dz[:, blk] + fade * (nn(bb, ghi) + nn(bb, glo))
        dy = dyhi[:, blk].astype(F32) + dylo[:, blk].astype(F32)
        gx_ref[:, blk] = (nn_hi(sk8, e1)[0:1] * dy + sb * dzb).astype(BF16)
        xdz = x * dzb
        hi, lo = split(xdz)
        p2[...] += nt(e1b, hi) + nt(e1b, lo)
        hi, lo = split(yv[:, blk] * dy - sb * xdz)
        p1[...] += nt(e1b, hi) + nt(e1b, lo)
        hi, lo = split(fade * sb * x)
        gb_ref[...] += nt(hi, ghi) + nt(lo, ghi) + nt(hi, glo)
        s_last = jnp.exp2(last) * s_in[:, blk] + local_f[:, blk]
        row_d[:, blk] = jnp.broadcast_to(jnp.sum(x * dy, axis=0, keepdims=True), (8, 128))
        row_b[:, blk] = jnp.broadcast_to(jnp.sum(grad * s_last, axis=0, keepdims=True), (8, 128))

    heads = (iota((H, HP), 0) == iota((H, HP), 1) // PS).astype(F32)
    edge_h = nt_hi(heads, row_b[...])[:, 0:1]
    skip_h = nt_hi(row_d[...], heads)
    later = (iota((T, T), 0) >= iota((T, T), 1)).astype(F32)
    dld = nn_hi(p1[...], later) + edge_h
    gdt = (rate * dld + p2[...]) * sg_ref[...]
    gdt_ref[...] = gdt
    ones8 = jnp.ones((8, T), F32)
    log_h = nt_hi(ones8, dld * ld_ref[...])
    bias_h = nt_hi(ones8, gdt)
    hsum[...] = jnp.zeros_like(hsum)
    hsum[:, 0:H] = jnp.where(rows8 == 0, log_h, jnp.where(rows8 == 1, skip_h, bias_h))

    @pl.loop(1, G1)
    def _(k):
        j = lax.rem(low + k, G1)
        remote(hsum, hgot1.at[low], 16, 16, group * G1 + j).start()

    hgot1[low] = hsum[...]
    arrived(hgot1, G1 - 1, 16)
    hmid[...] = jnp.sum(hgot1[...], axis=0)
    spot = me_dp * (nf // G1) + group

    @pl.loop(1, g2n)
    def _(k):
        j = lax.rem(spot + k, g2n)
        remote(
            hmid, hgot2.at[spot], 17, 17, j % (nf // G1) * G1 + low, j // (nf // G1)
        ).start()

    hgot2[spot] = hmid[...]
    arrived(hgot2, g2n - 1, 17)
    hg_ref[...] = jnp.sum(hgot2[...], axis=0)


def on_device(dp_n, nf, layer_in, in_b, in_c, dt_raw, a_log, skip_gain, dt_bias, foot_map, contact, out_grad):
    chips = nf // 2
    lanes = HP // (chips // 8)
    vm = lambda *shape: pltpu.VMEM(shape, F32)
    vb = lambda *shape: pltpu.VMEM(shape, BF16)
    whole = pl.BlockSpec(memory_space=pltpu.VMEM)
    gx, gb, gc, gdt, hg = pl.pallas_call(
        functools.partial(kernel, dp_n, nf),
        out_shape=(
            jax.ShapeDtypeStruct((T, HP), BF16),
            jax.ShapeDtypeStruct((T, N), F32),
            jax.ShapeDtypeStruct((T, N), F32),
            jax.ShapeDtypeStruct((H, T), F32),
            jax.ShapeDtypeStruct((8, 128), F32),
        ),
        in_specs=[whole] * 10,
        out_specs=[whole] * 5,
        scratch_shapes=[
            vm(N, HP),
            vm(N, HP),
            vm(N, HP),
            vm(N, HP),
            vm(N // 2, HP),
            vm(N // 2, HP),
            vm(chips, 8, lanes),
            vm(chips, 8, lanes),
            vm(chips, 8, lanes),
            vm(chips, 8, lanes),
            vm(N, HP),
            vm(N, HP),
            vm(T, HP),
            vm(T, HP),
            vm(T, HP),
            vm(T, HP),
            vb(T, HP),
            vb(T, HP),
            vb(T, HP),
            vb(T, HP),
            vm(128, HP),
            vm(PAIRS, 8, T),
            vm(H, T),
            vm(H, T),
            vm(T, T),
            vm(T, T),
            vm(128, T),
            vm(128, 128),
            vm(8, 128),
            vm(nf, 8, 128),
            vm(8, 128),
            vm(nf, 128),
            vm(T, 128),
            vm(8, 128),
            vm(8, 128),
            vm(N, KL),
            vm(nf, 8, 128),
            vm(nf, 8, 128),
            vm(N, KL),
            vm(H, T),
            vm(H, T),
            vm(8, HP),
            vm(8, HP),
            vm(8, 128),
            vm(G1, 8, 128),
            vm(8, 128),
            vm(dp_n * (nf // G1), 8, 128),
            pltpu.SemaphoreType.DMA((18,)),
            pltpu.SemaphoreType.DMA((18,)),
        ],
        compiler_params=pltpu.CompilerParams(
            collective_id=0, has_side_effects=True, vmem_limit_bytes=56 * 2**20
        ),
    )(
        layer_in[0],
        in_b[0],
        in_c[0],
        dt_raw[0],
        a_log[None],
        skip_gain[None],
        dt_bias[None],
        foot_map,
        contact,
        out_grad[0],
    )
    return gx[None], gb[None], gc[None], gdt[None], hg[0:3, 0:H]


def solution(mesh):
    return jax.shard_map(
        functools.partial(on_device, mesh.shape["dp"], mesh.shape["frame"]),
        mesh=mesh,
        in_specs=(
            P("dp", "frame", None),
            P("dp", "frame", None),
            P("dp", "frame", None),
            P("dp", None, "frame"),
            P(),
            P(),
            P(),
            P(),
            P("dp", "frame"),
            P("dp", "frame", None),
        ),
        out_specs=(
            P("dp", "frame", None),
            P("dp", "frame", None),
            P("dp", "frame", None),
            P("dp", None, "frame"),
            P(),
        ),
        check_vma=False,
    )
```

```python
import functools

import jax
import jax.numpy as jnp
from jax import lax
from jax.experimental import pallas as pl
from jax.experimental.pallas import tpu as pltpu
from jax.sharding import PartitionSpec as P

MESH = pl.DeviceIdType.MESH
HIGH = lax.Precision.HIGHEST
F32, BF16 = jnp.float32, jnp.bfloat16
H, PS, N, T, HP, FEET = 32, 64, 128, 256, 2048, 12
PAIRS = HP // 128
LOG2E = 1.4426950408889634
KL = 512
WB = 256
BLOCKS = HP // WB
G1 = 16


def nn(a, b):
    return lax.dot_general(a, b, (((1,), (0,)), ((), ())), preferred_element_type=F32)


def nt(a, b):
    return lax.dot_general(a, b, (((1,), (1,)), ((), ())), preferred_element_type=F32)


def nn_hi(a, b):
    return lax.dot_general(
        a, b, (((1,), (0,)), ((), ())), precision=HIGH, preferred_element_type=F32
    )


def nt_hi(a, b):
    return lax.dot_general(
        a, b, (((1,), (1,)), ((), ())), precision=HIGH, preferred_element_type=F32
    )


def split(v):
    hi = v.astype(BF16)
    return hi, (v - hi.astype(F32)).astype(BF16)


def split3(v):
    hi = v.astype(BF16)
    rest = v - hi.astype(F32)
    mid = rest.astype(BF16)
    return hi, mid, (rest - mid.astype(F32)).astype(BF16)


def iota(shape, dim):
    return lax.broadcasted_iota(jnp.int32, shape, dim)


def kernel(
    dp_n,
    nf,
    x_ref,
    b_ref,
    c_ref,
    dt_ref,
    al_ref,
    sk_ref,
    bi_ref,
    f_ref,
    ct_ref,
    og_ref,
    gx_ref,
    gb_ref,
    gc_ref,
    gdt_ref,
    hg_ref,
    local_f,
    local_r,
    sib_f,
    sib_r,
    half_f,
    half_r,
    got_f,
    got_r,
    ret_f,
    ret_r,
    s_in,
    g_end,
    cexp,
    sexp,
    yv,
    dz,
    zhi,
    zlo,
    dyhi,
    dylo,
    whi,
    wlo,
    bhi,
    blo,
    f48,
    e96,
    row_sk,
    row_sib,
    c2_ref,
    ld_ref,
    step_ref,
    sg_ref,
    sc_ref,
    sct_ref,
    ds0,
    ds1,
    dec_mine,
    dec_row,
    decs,
    sib_dec,
    dec_all,
    vel,
    vel_prev,
    vel_next,
    gd_local,
    gd_sib,
    gd_half,
    gd_got,
    gd_ret,
    gd_end,
    p1,
    p2,
    row_d,
    row_b,
    hsum,
    hgot1,
    hmid,
    hgot2,
    ssem,
    rsem,
):
    chips = nf // 2
    me_dp = lax.axis_index("dp")
    me = lax.axis_index("frame")
    chip, core = me // 2, me % 2
    sib = me + 1 - 2 * core
    first = core == 0
    lbs = chips // 8
    lanes = HP // lbs
    halves = chips // G1
    g2n = dp_n * halves * 2
    group, low = chip // G1, chip % G1
    spot = (me_dp * halves + group) * 2 + core

    def ring(k, base=None):
        return lax.rem(me + k, nf)

    barrier = pltpu.get_barrier_semaphore()

    def greet(frame, dp=None):
        pl.semaphore_signal(
            barrier,
            inc=1,
            device_id=(me_dp if dp is None else dp, frame),
            device_id_type=MESH,
        )

    def second(k):
        j = lax.rem(spot + k, g2n)
        return (j // 2 % halves * G1 + low) * 2 + j % 2, j // (2 * halves)

    greet(sib)
    greet(lax.rem(me + nf - 1 + 2 * core, nf))

    @pl.loop(1, chips)
    def _(k):
        greet(lax.rem(chip + k, chips) * 2 + core)

    @pl.loop(1, g2n)
    def _(k):
        greet(*second(k))

    def remote(src, dst, s, r, dev, dp=None):
        return pltpu.make_async_remote_copy(
            src_ref=src,
            dst_ref=dst,
            send_sem=ssem.at[s],
            recv_sem=rsem.at[r],
            device_id=(me_dp if dp is None else dp, dev),
            device_id_type=MESH,
        )

    def arrived(buf, n, s):
        view = buf.at[pl.ds(0, n)]
        d = remote(view, view, s, s, sib)
        d.wait()

    eye = (iota((T, T), 0) == iota((T, T), 1)).astype(F32)
    rows8 = iota((8, H), 0)
    rows = jnp.where(
        rows8 == 0, al_ref[...], jnp.where(rows8 == 1, sk_ref[...], bi_ref[...])
    )
    eye32 = (iota((H, H), 0) == iota((H, H), 1)).astype(F32)
    cols = nt_hi(eye32, rows)
    rate = -jnp.exp(cols[:, 0:1])
    raw = dt_ref[...] + cols[:, 2:3]
    tail = jnp.exp(-jnp.abs(raw))
    step = jnp.maximum(raw, 0.0) + jnp.log1p(tail)
    sg_ref[...] = jnp.where(raw >= 0, 1.0, tail) / (1.0 + tail)
    ld = rate * step
    ld_ref[...] = ld
    step_ref[...] = step
    upper = (iota((T, T), 0) <= iota((T, T), 1)).astype(F32)
    c2 = nn_hi(ld, upper) * LOG2E
    for i in range(PAIRS):
        c2_ref[i, 0:2, :] = c2[2 * i : 2 * i + 2]
    c3 = jnp.concatenate(split3(nt_hi(eye, c2)), axis=1)
    s3 = jnp.concatenate(split3(nt_hi(eye, step)), axis=1)
    spread_k = (iota((96, KL), 0) % H == iota((96, KL), 1) % H).astype(BF16)
    c_feet = nn(c3, spread_k)
    dec_mine[...] = jnp.broadcast_to(c_feet[T - 1 : T, 0:128], (8, 128))
    eye_b = (iota((N, N), 0) == iota((N, N), 1)).astype(BF16)
    bb, cc = b_ref[...], c_ref[...]
    bt = nt(eye_b, bb).astype(BF16)
    ct = nt(eye_b, cc).astype(BF16)

    fhi, flo = split(jnp.concatenate([f_ref[...], jnp.zeros((4, HP), F32)], axis=0))
    f48[...] = jnp.concatenate([fhi, flo, fhi], axis=0)
    e96[...] = (iota((96, HP), 0) % H == iota((96, HP), 1) // PS).astype(BF16)
    sk8 = jnp.broadcast_to(sk_ref[...], (8, H))
    row_sk[...] = nn(jnp.concatenate(split3(sk8), axis=1), e96[...])

    def block(i):
        return pl.ds(pl.multiple_of(i * WB, WB), WB)

    @pl.loop(0, BLOCKS, unroll=2)
    def _(i):
        blk = block(i)
        e3 = e96[:, blk]
        cb, sb = nn(c3, e3), nn(s3, e3)
        cexp[:, blk] = cb
        sexp[:, blk] = sb
        z = sb * x_ref[:, blk].astype(F32)
        hi, lo = split(z)
        zhi[:, blk] = hi
        zlo[:, blk] = lo
        hi, lo = split(jnp.exp2(cb[T - 1 : T] - cb) * z)
        whi[:, blk] = hi
        wlo[:, blk] = lo
        local_f[:, blk] = nn(bt, hi) + nn(bt, lo)

    pl.semaphore_wait(barrier, chips + g2n)

    mine_half = pl.ds(pl.multiple_of(core * 64, 64), 64)
    sib_half = pl.ds(pl.multiple_of(64 - core * 64, 64), 64)
    ex_dec = remote(dec_mine, sib_dec, 5, 5, sib)
    ex = [
        remote(local_f.at[sib_half], sib_f.at[sib_half], 1, 1, sib),
        remote(local_r.at[sib_half], sib_r.at[sib_half], 2, 2, sib),
        remote(local_f.at[mine_half], sib_f.at[mine_half], 3, 3, sib),
        remote(local_r.at[mine_half], sib_r.at[mine_half], 4, 4, sib),
    ]
    ex_dec.start()
    ex[0].start()

    def reverse(i):
        blk = block(i)
        hi, lo = split(jnp.exp2(cexp[:, blk]) * og_ref[:, blk].astype(F32))
        local_r[:, blk] = nn(ct, hi) + nn(ct, lo)

    pl.loop(0, BLOCKS // 2, unroll=2)(reverse)
    ex_dec.wait()
    row_sib[...] = jnp.exp2(
        nn(jnp.concatenate(split3(sib_dec[:, 0:H]), axis=1), e96[...])
    )
    ex[0].wait()

    def part(o):
        return (
            pl.ds(pl.multiple_of(o // lbs * 8, 8), 8),
            pl.ds(pl.multiple_of(o % lbs * lanes, 128), lanes),
        )

    my_r, my_l = part(chip)

    @pl.loop(0, BLOCKS)
    def _(i):
        blk = block(i)
        d_sib = row_sib[0:1, blk]
        d_me = jnp.exp2(cexp[T - 8 : T, blk])[7:8]
        one = jnp.ones_like(d_me)
        half_f[:, blk] = (
            jnp.where(first, d_sib, one) * local_f[mine_half, blk]
            + jnp.where(first, one, d_me) * sib_f[mine_half, blk]
        )

    @pl.loop(1, chips)
    def _(k):
        o = lax.rem(chip + k, chips)
        r, l = part(o)
        remote(half_f.at[r, l], got_f.at[chip], 6, 6, o * 2 + core).start()

    got_f[chip] = half_f[my_r, my_l]
    dec_row[...] = dec_mine[0:1] + sib_dec[0:1]
    decs[chip] = dec_row[...]
    pl.loop(BLOCKS // 2, BLOCKS, unroll=2)(reverse)
    ex[1].start()
    ex[2].start()
    ex[3].start()

    @pl.loop(1, chips)
    def _(k):
        o = lax.rem(chip + k, chips)
        remote(dec_row, decs.at[chip], 0, 0, o * 2 + core).start()

    scores = nt(cc, bb)
    sc_ref[...] = jnp.where(iota((T, T), 0) >= iota((T, T), 1), scores, 0.0)
    scores = nt(bb, cc)
    sct_ref[...] = jnp.where(iota((T, T), 0) <= iota((T, T), 1), scores, 0.0)

    low_lanes = iota((128, 128), 1) < PS

    def inner(i):
        blk = pl.ds(pl.multiple_of(i * 128, 128), 128)
        rhs = jnp.concatenate([zhi[:, blk], zlo[:, blk]], axis=1)
        cb = cexp[:, blk]
        for r in range(2):
            seen = 128 * (r + 1)
            at = slice(128 * r, seen)
            outs = []
            for e in range(2):
                col = cb[at, PS * e : PS * e + 1]
                row = c2_ref[i, e : e + 1, 0:seen]
                mix = sc_ref[at, 0:seen] * jnp.exp2(jnp.minimum(col - row, 0.0))
                hi, lo = split(mix)
                res = nn(hi, rhs[0:seen]) + nn(lo, rhs[0:seen])
                outs.append(res[:, 0:128] + res[:, 128:256])
            yv[at, blk] = jnp.where(low_lanes, outs[0], outs[1])

    pl.loop(0, 3)(inner)
    ex[1].wait()

    @pl.loop(0, BLOCKS)
    def _(i):
        blk = block(i)
        d_sib = row_sib[0:1, blk]
        d_me = jnp.exp2(cexp[T - 8 : T, blk])[7:8]
        one = jnp.ones_like(d_me)
        half_r[:, blk] = (
            jnp.where(first, one, d_sib) * local_r[mine_half, blk]
            + jnp.where(first, d_me, one) * sib_r[mine_half, blk]
        )

    got_r[chip] = half_r[my_r, my_l]

    pl.loop(3, 9)(inner)
    arrived(decs, chips - 1, 0)
    dall = decs[:, 0, :]
    dec_all[...] = jnp.exp2(dall)
    head0 = chip % lbs * (lanes // PS)
    spread_l = (iota((128, lanes), 0) == head0 + iota((128, lanes), 1) // PS).astype(F32)
    chip_dec = jnp.exp2(nn_hi(dall, spread_l))

    arrived(got_f, chips - 1, 6)
    acc = jnp.zeros((8, lanes), F32)
    for q in range(chips):
        ret_f[q] = acc
        acc = got_f[q] + chip_dec[q : q + 1] * acc

    @pl.loop(1, chips)
    def _(k):
        o = lax.rem(chip + k, chips)
        r = pl.ds(pl.multiple_of(core * 64 + chip // lbs * 8, 8), 8)
        remote(ret_f.at[o], s_in.at[r, my_l], 8, 8, o * 2 + core).start()

    own = pl.ds(pl.multiple_of(core * 64 + chip // lbs * 8, 8), 8)
    s_in[own, my_l] = ret_f[chip]
    pl.loop(9, PAIRS)(inner)

    @pl.loop(0, BLOCKS)
    def _(i):
        blk = block(i)
        eh = e96[0:H, blk]
        fhi, flo = f48[0:16, blk], f48[16:32, blk]
        for k in range(FEET):
            rows_k = slice(k * H, k * H + H)
            bhi[rows_k, blk] = jnp.where(eh > 0, jnp.broadcast_to(fhi[k : k + 1], eh.shape), 0.0).astype(BF16)
            blo[rows_k, blk] = jnp.where(eh > 0, jnp.broadcast_to(flo[k : k + 1], eh.shape), 0.0).astype(BF16)

    ex[2].wait()
    ex[3].wait()
    arrived(ret_f, chips - 1, 8)
    back_f = remote(s_in.at[mine_half], s_in.at[mine_half], 10, 10, sib)
    back_f.start()

    @pl.loop(1, chips)
    def _(k):
        o = lax.rem(chip + k, chips)
        r, l = part(o)
        remote(half_r.at[r, l], got_r.at[chip], 7, 7, o * 2 + core).start()

    back_f.wait()

    vel[...] = jnp.zeros_like(vel)

    @pl.loop(0, BLOCKS, unroll=2)
    def _(i):
        blk = block(i)
        state = s_in[:, blk]
        state = jnp.where(first, state, sib_f[:, blk] + row_sib[0:1, blk] * state)
        s_in[:, blk] = state
        hi, lo = split(state)
        y = yv[:, blk] + jnp.exp2(cexp[:, blk]) * (nn(cc, hi) + nn(cc, lo))
        yv[:, blk] = y
        hi, lo = split(y + row_sk[0:1, blk] * x_ref[:, blk].astype(F32))
        both = nt(hi, f48[0:32, blk])
        vel[:, 0:16] += both[:, 0:16] + both[:, 16:32] + nt(lo, f48[0:16, blk])

    touch = jnp.broadcast_to(ct_ref[...].astype(F32), (8, T))
    touch = nt_hi(eye, touch)[:, 0:1]
    lane = iota((T, 128), 1)
    row = iota((T, 128), 0)
    v = jnp.where(lane == FEET, touch, vel[...])
    vel[...] = v
    to_next = remote(vel.at[pl.ds(T - 8, 8)], vel_prev, 12, 12, ring(1))
    to_prev = remote(vel.at[pl.ds(0, 8)], vel_next, 13, 13, ring(nf - 1))
    to_next.start()
    to_prev.start()
    to_next.wait()
    to_prev.wait()
    feet = lane < FEET
    before = jnp.where(row == 0, vel_prev[7:8, :], pltpu.roll(v, 1, 0))
    slide = jnp.where(
        feet & ((row > 0) | (me > 0)), touch * (v - before), 0.0
    )
    nxt = vel_next[0:1, :]
    edge = nxt[:, FEET : FEET + 1] * (nxt - v[T - 1 : T, :])
    edge = jnp.where((iota((1, 128), 1) < FEET) & (me < nf - 1), edge, 0.0)
    change = slide - jnp.where(row == T - 1, edge, pltpu.roll(slide, T - 1, 0))
    chi, clo = split(change)

    feet_of = (iota((128, KL), 0) == iota((128, KL), 1) // H).astype(BF16)
    hi, lo = split(jnp.exp2(c_feet) * (nn(chi, feet_of) + nn(clo, feet_of)))
    gd_local[...] = nn(ct, hi) + nn(ct, lo)

    gd_ex = remote(gd_local, gd_sib, 18, 18, sib)
    gd_ex.start()

    def tile(o, base):
        return (
            pl.ds(pl.multiple_of(base + o // 4 * 8, 8), 8),
            pl.ds(pl.multiple_of(o % 4 * 128, 128), 128),
        )

    c48 = jnp.concatenate([chi[:, 0:16], chi[:, 0:16], clo[:, 0:16]], axis=1)

    def total_grad(i):
        blk = block(i)
        hi, lo = split(og_ref[:, blk].astype(F32) + nn(c48, f48[:, blk]))
        dyhi[:, blk] = hi
        dylo[:, blk] = lo

    pl.loop(0, BLOCKS // 2, unroll=2)(total_grad)
    gd_ex.wait()
    decay_me = jnp.exp2(jnp.concatenate([dec_mine[0:1]] * 4, axis=1))
    decay_sib = jnp.exp2(jnp.concatenate([sib_dec[0:1]] * 4, axis=1))
    one = jnp.ones_like(decay_me)
    gd_half[...] = (
        jnp.where(first, one, decay_sib) * gd_local[mine_half, :]
        + jnp.where(first, decay_me, one) * gd_sib[mine_half, :]
    )

    @pl.loop(1, chips)
    def _(k):
        o = lax.rem(chip + k, chips)
        r, l = tile(o, 0)
        remote(gd_half.at[r, l], gd_got.at[chip], 14, 14, o * 2 + core).start()

    gd_r, gd_l = tile(chip, 0)
    gd_got[chip] = gd_half[gd_r, gd_l]
    gd_r, gd_l = tile(chip, core * 64)
    pl.loop(BLOCKS // 2, BLOCKS, unroll=2)(total_grad)
    arrived(got_r, chips - 1, 7)
    acc = jnp.zeros((8, lanes), F32)
    for q in reversed(range(chips)):
        ret_r[q] = acc
        acc = got_r[q] + chip_dec[q : q + 1] * acc

    @pl.loop(1, chips)
    def _(k):
        o = lax.rem(chip + k, chips)
        r = pl.ds(pl.multiple_of(core * 64 + chip // lbs * 8, 8), 8)
        remote(ret_r.at[o], g_end.at[r, my_l], 9, 9, o * 2 + core).start()

    g_end[own, my_l] = ret_r[chip]

    ds0[...] = jnp.zeros_like(ds0)
    ds1[...] = jnp.zeros_like(ds1)
    zero_b = jnp.zeros((128, 128), BF16)

    def backward(i):
        blk = pl.ds(pl.multiple_of(i * 128, 128), 128)
        dh, dl = dyhi[:, blk], dylo[:, blk]
        rhs = jnp.concatenate([dh, dl], axis=1)
        twice = jnp.concatenate([dh, dh], axis=1)
        cb = cexp[:, blk]
        for r, acc in ((0, ds0), (1, ds1)):
            at, on = slice(128 * r, 128 * r + 128), slice(128 * r, T)
            zh, zl = zhi[at, blk], zlo[at, blk]
            outs = []
            total = acc[...]
            for e in range(2):
                keep = low_lanes if e == 0 else ~low_lanes
                zhe = jnp.where(keep, zh, zero_b)
                zle = jnp.where(keep, zl, zero_b)
                col = cb[at, PS * e : PS * e + 1]
                fall = jnp.exp2(jnp.minimum(c2_ref[i, e : e + 1, on] - col, 0.0))
                w = nt(jnp.concatenate([zhe, zle], axis=1), twice[on]) + nt(zhe, dl[on])
                total = total + fall * w
                hi, lo = split(sct_ref[at, on] * fall)
                res = nn(hi, rhs[on]) + nn(lo, rhs[on])
                outs.append(res[:, 0:128] + res[:, 128:256])
            acc[...] = total
            dz[at, blk] = jnp.where(low_lanes, outs[0], outs[1])

    pl.loop(0, 5)(backward)

    arrived(gd_got, chips - 1, 14)
    acc = jnp.zeros((8, 128), F32)
    for q in reversed(range(chips)):
        gd_ret[q] = acc
        acc = gd_got[q] + dec_all[q : q + 1] * acc

    @pl.loop(1, chips)
    def _(k):
        o = lax.rem(chip + k, chips)
        remote(gd_ret.at[o], gd_end.at[gd_r, gd_l], 15, 15, o * 2 + core).start()

    gd_end[gd_r, gd_l] = gd_ret[chip]
    pl.loop(5, PAIRS)(backward)

    m0 = iota((128, T), 0) <= iota((128, T), 1)
    m1 = iota((128, 128), 0) <= iota((128, 128), 1)
    dst = jnp.concatenate(
        [
            jnp.where(m0, ds0[...], 0.0),
            jnp.concatenate(
                [jnp.zeros((128, 128), F32), jnp.where(m1, ds1[...], 0.0)], axis=1
            ),
        ],
        axis=0,
    )
    hi, lo = split(dst)
    gb_ref[...] = nn(hi, cc) + nn(lo, cc)
    p1[...] = jnp.zeros_like(p1)
    eye_t = eye.astype(BF16)
    hi = nt(eye_t, hi).astype(BF16)
    lo = nt(eye_t, lo).astype(BF16)
    gc_ref[...] = nn(hi, bb) + nn(lo, bb)

    @pl.loop(0, BLOCKS, unroll=2)
    def _(i):
        blk = block(i)
        dy = dyhi[:, blk].astype(F32) + dylo[:, blk].astype(F32)
        hi, lo = split(jnp.exp2(cexp[:, blk]) * dy)
        shi, slo = split(s_in[:, blk])
        gc_ref[...] += nt(hi, shi) + nt(lo, shi) + nt(hi, slo)
        x = x_ref[:, blk].astype(F32)
        hi, lo = split(yv[:, blk] * dy)
        eh = e96[0:H, blk]
        p1[...] += nt(eh, hi) + nt(eh, lo)
        row_d[:, blk] = jnp.broadcast_to(jnp.sum(x * dy, axis=0, keepdims=True), (8, WB))

    arrived(ret_r, chips - 1, 9)
    back_r = remote(g_end.at[mine_half], g_end.at[mine_half], 11, 11, sib)
    back_r.start()
    arrived(gd_ret, chips - 1, 15)
    gd_back = remote(gd_end.at[mine_half], gd_end.at[mine_half], 19, 19, sib)
    gd_back.start()
    gd_back.wait()
    back_r.wait()

    p2[...] = jnp.zeros_like(p2)
    gd_all = gd_end[...]
    gd_all = jnp.where(first, gd_sib[...] + decay_sib * gd_all, gd_all)
    gdh, gdl = split(gd_all[:, 0 : FEET * H])

    @pl.loop(0, BLOCKS, unroll=2)
    def _(i):
        blk = block(i)
        eh = e96[0:H, blk]
        grad = g_end[:, blk]
        grad = jnp.where(first, sib_r[:, blk] + row_sib[0:1, blk] * grad, grad)
        grad = grad + nn(gdh, bhi[:, blk]) + nn(gdl, bhi[:, blk]) + nn(gdh, blo[:, blk])
        g_end[:, blk] = grad
        ghi, glo = split(grad)
        cb = cexp[:, blk]
        last = cb[T - 1 : T]
        dzb = dz[:, blk] + jnp.exp2(last - cb) * (nn(bb, ghi) + nn(bb, glo))
        dz[:, blk] = dzb
        xdz = x_ref[:, blk].astype(F32) * dzb
        hi, lo = split(xdz)
        p2[...] += nt(eh, hi) + nt(eh, lo)
        s_last = jnp.exp2(last) * s_in[:, blk] + local_f[:, blk]
        row_b[:, blk] = jnp.broadcast_to(jnp.sum(grad * s_last, axis=0, keepdims=True), (8, WB))

    heads = (iota((H, HP), 0) == iota((H, HP), 1) // PS).astype(F32)
    edge_h = nt_hi(heads, row_b[...])[:, 0:1]
    skip_h = nt_hi(row_d[...], heads)
    later = (iota((T, T), 0) >= iota((T, T), 1)).astype(F32)
    dld = nn_hi(p1[...] - step_ref[...] * p2[...], later) + edge_h
    gdt = (rate * dld + p2[...]) * sg_ref[...]
    gdt_ref[...] = gdt
    ones8 = jnp.ones((8, T), F32)
    log_h = nt_hi(ones8, dld * ld_ref[...])
    bias_h = nt_hi(ones8, gdt)
    hsum[...] = jnp.zeros_like(hsum)
    hsum[:, 0:H] = jnp.where(rows8 == 0, log_h, jnp.where(rows8 == 1, skip_h, bias_h))

    @pl.loop(1, G1)
    def _(k):
        j = lax.rem(low + k, G1)
        remote(hsum, hgot1.at[low], 16, 16, (group * G1 + j) * 2 + core).start()

    hgot1[low] = hsum[...]

    def sources(i):
        blk = block(i)
        dy = dyhi[:, blk].astype(F32) + dylo[:, blk].astype(F32)
        gx_ref[:, blk] = (row_sk[0:1, blk] * dy + sexp[:, blk] * dz[:, blk]).astype(BF16)
        hi, lo = whi[:, blk], wlo[:, blk]
        ghi, glo = split(g_end[:, blk])
        gb_ref[...] += nt(hi, ghi) + nt(lo, ghi) + nt(hi, glo)

    pl.loop(0, BLOCKS // 2, unroll=2)(sources)
    arrived(hgot1, G1 - 1, 16)
    hmid[...] = jnp.sum(hgot1[...], axis=0)

    @pl.loop(1, g2n)
    def _(k):
        frame, dp = second(k)
        remote(hmid, hgot2.at[spot], 17, 17, frame, dp).start()

    hgot2[spot] = hmid[...]
    pl.loop(BLOCKS // 2, BLOCKS, unroll=2)(sources)
    arrived(hgot2, g2n - 1, 17)
    hg_ref[...] = jnp.sum(hgot2[...], axis=0)


def hand_out(gx, gb, gc, gdt, hg, gx_o, gb_o, gc_o, gdt_o, hg_o, sem):
    pairs = ((gx, gx_o), (gb, gb_o), (gc, gc_o), (gdt, gdt_o))
    copies = [
        pltpu.make_async_copy(a, b.at[0], sem.at[k]) for k, (a, b) in enumerate(pairs)
    ]
    for copy in copies:
        copy.start()
    hg_o[...] = hg[0:3, 0:H]
    for copy in copies:
        copy.wait()


def on_device(dp_n, nf, layer_in, in_b, in_c, dt_raw, a_log, skip_gain, dt_bias, foot_map, contact, out_grad):
    chips = nf // 2
    lanes = HP // (chips // 8)
    vm = lambda *shape: pltpu.VMEM(shape, F32)
    vb = lambda *shape: pltpu.VMEM(shape, BF16)
    whole = pl.BlockSpec(memory_space=pltpu.VMEM)
    gx, gb, gc, gdt, hg = pl.pallas_call(
        functools.partial(kernel, dp_n, nf),
        out_shape=(
            jax.ShapeDtypeStruct((T, HP), BF16),
            jax.ShapeDtypeStruct((T, N), F32),
            jax.ShapeDtypeStruct((T, N), F32),
            jax.ShapeDtypeStruct((H, T), F32),
            jax.ShapeDtypeStruct((8, 128), F32),
        ),
        in_specs=[whole] * 10,
        out_specs=[whole] * 5,
        scratch_shapes=[
            vm(N, HP),
            vm(N, HP),
            vm(N, HP),
            vm(N, HP),
            vm(N // 2, HP),
            vm(N // 2, HP),
            vm(chips, 8, lanes),
            vm(chips, 8, lanes),
            vm(chips, 8, lanes),
            vm(chips, 8, lanes),
            vm(N, HP),
            vm(N, HP),
            vm(T, HP),
            vm(T, HP),
            vm(T, HP),
            vm(T, HP),
            vb(T, HP),
            vb(T, HP),
            vb(T, HP),
            vb(T, HP),
            vb(T, HP),
            vb(T, HP),
            vb(FEET * H, HP),
            vb(FEET * H, HP),
            vb(48, HP),
            vb(96, HP),
            vm(8, HP),
            vm(8, HP),
            vm(PAIRS, 8, T),
            vm(H, T),
            vm(H, T),
            vm(H, T),
            vm(T, T),
            vm(T, T),
            vm(128, T),
            vm(128, 128),
            vm(8, 128),
            vm(1, 128),
            vm(chips, 1, 128),
            vm(8, 128),
            vm(chips, 128),
            vm(T, 128),
            vm(8, 128),
            vm(8, 128),
            vm(N, KL),
            vm(N, KL),
            vm(N // 2, KL),
            vm(chips, 8, 128),
            vm(chips, 8, 128),
            vm(N, KL),
            vm(H, T),
            vm(H, T),
            vm(8, HP),
            vm(8, HP),
            vm(8, 128),
            vm(G1, 8, 128),
            vm(8, 128),
            vm(dp_n * (nf // G1), 8, 128),
            pltpu.SemaphoreType.DMA((20,)),
            pltpu.SemaphoreType.DMA((20,)),
        ],
        compiler_params=pltpu.CompilerParams(
            collective_id=0, has_side_effects=True, vmem_limit_bytes=56 * 2**20
        ),
    )(
        layer_in[0],
        in_b[0],
        in_c[0],
        dt_raw[0],
        a_log[None],
        skip_gain[None],
        dt_bias[None],
        foot_map,
        contact,
        out_grad[0],
    )
    place = pl.BlockSpec(memory_space=pl.ANY)
    return pl.pallas_call(
        hand_out,
        out_shape=(
            jax.ShapeDtypeStruct((1, T, HP), BF16),
            jax.ShapeDtypeStruct((1, T, N), F32),
            jax.ShapeDtypeStruct((1, T, N), F32),
            jax.ShapeDtypeStruct((1, H, T), F32),
            jax.ShapeDtypeStruct((3, H), F32),
        ),
        in_specs=[whole] * 5,
        out_specs=[place] * 4 + [whole],
        scratch_shapes=[pltpu.SemaphoreType.DMA((4,))],
    )(gx, gb, gc, gdt, hg)


def solution(mesh):
    return jax.shard_map(
        functools.partial(on_device, mesh.shape["dp"], mesh.shape["frame"]),
        mesh=mesh,
        in_specs=(
            P("dp", "frame", None),
            P("dp", "frame", None),
            P("dp", "frame", None),
            P("dp", None, "frame"),
            P(),
            P(),
            P(),
            P(),
            P("dp", "frame"),
            P("dp", "frame", None),
        ),
        out_specs=(
            P("dp", "frame", None),
            P("dp", "frame", None),
            P("dp", "frame", None),
            P("dp", None, "frame"),
            P(),
        ),
        check_vma=False,
    )
```

```python
import functools

import jax
import jax.numpy as jnp
from jax import lax
from jax.experimental import pallas as pl
from jax.experimental.pallas import tpu as pltpu
from jax.sharding import PartitionSpec as P

MESH = pl.DeviceIdType.MESH
HIGH = lax.Precision.HIGHEST
F32, BF16 = jnp.float32, jnp.bfloat16
H, PS, N, T, HP, FEET = 32, 64, 128, 256, 2048, 12
PAIRS = HP // 128
LOG2E = 1.4426950408889634
KL = 512
WB = 256
BLOCKS = HP // WB
G1 = 16


def nn(a, b):
    return lax.dot_general(a, b, (((1,), (0,)), ((), ())), preferred_element_type=F32)


def nt(a, b):
    return lax.dot_general(a, b, (((1,), (1,)), ((), ())), preferred_element_type=F32)


def nn_hi(a, b):
    return lax.dot_general(
        a, b, (((1,), (0,)), ((), ())), precision=HIGH, preferred_element_type=F32
    )


def nt_hi(a, b):
    return lax.dot_general(
        a, b, (((1,), (1,)), ((), ())), precision=HIGH, preferred_element_type=F32
    )


def split(v):
    hi = v.astype(BF16)
    return hi, (v - hi.astype(F32)).astype(BF16)


def split3(v):
    hi = v.astype(BF16)
    rest = v - hi.astype(F32)
    mid = rest.astype(BF16)
    return hi, mid, (rest - mid.astype(F32)).astype(BF16)


def iota(shape, dim):
    return lax.broadcasted_iota(jnp.int32, shape, dim)


def kernel(
    dp_n,
    nf,
    x_ref,
    b_ref,
    c_ref,
    dt_ref,
    al_ref,
    sk_ref,
    bi_ref,
    f_ref,
    ct_ref,
    og_ref,
    gx_ref,
    gb_ref,
    gc_ref,
    gdt_ref,
    hg_ref,
    local_f,
    local_r,
    sib_f,
    sib_r,
    half_f,
    half_r,
    got_f,
    got_r,
    ret_f,
    ret_r,
    s_in,
    g_end,
    cexp,
    sexp,
    yv,
    dz,
    zhi,
    zlo,
    dyhi,
    dylo,
    whi,
    wlo,
    bhi,
    blo,
    f48,
    e96,
    row_sk,
    row_sib,
    c2_ref,
    ld_ref,
    step_ref,
    sg_ref,
    sc_ref,
    sct_ref,
    ds0,
    ds1,
    dec_mine,
    dec_row,
    decs,
    sib_dec,
    dec_all,
    vel,
    vel_prev,
    vel_next,
    gd_local,
    gd_sib,
    gd_half,
    gd_got,
    gd_ret,
    gd_end,
    p1,
    p2,
    row_d,
    row_b,
    hsum,
    hgot1,
    hmid,
    hgot2,
    ssem,
    rsem,
):
    chips = nf // 2
    me_dp = lax.axis_index("dp")
    me = lax.axis_index("frame")
    chip, core = me // 2, me % 2
    sib = me + 1 - 2 * core
    first = core == 0
    lbs = chips // 8
    lanes = HP // lbs
    halves = chips // G1
    g2n = dp_n * halves * 2
    group, low = chip // G1, chip % G1
    spot = (me_dp * halves + group) * 2 + core

    def ring(k, base=None):
        return lax.rem(me + k, nf)

    barrier = pltpu.get_barrier_semaphore()

    def greet(frame, dp=None):
        pl.semaphore_signal(
            barrier,
            inc=1,
            device_id=(me_dp if dp is None else dp, frame),
            device_id_type=MESH,
        )

    def second(k):
        j = lax.rem(spot + k, g2n)
        return (j // 2 % halves * G1 + low) * 2 + j % 2, j // (2 * halves)

    greet(sib)
    greet(lax.rem(me + nf - 1 + 2 * core, nf))

    @pl.loop(1, chips)
    def _(k):
        greet(lax.rem(chip + k, chips) * 2 + core)

    @pl.loop(1, g2n)
    def _(k):
        greet(*second(k))

    def remote(src, dst, s, r, dev, dp=None):
        return pltpu.make_async_remote_copy(
            src_ref=src,
            dst_ref=dst,
            send_sem=ssem.at[s],
            recv_sem=rsem.at[r],
            device_id=(me_dp if dp is None else dp, dev),
            device_id_type=MESH,
        )

    def arrived(buf, n, s):
        view = buf.at[pl.ds(0, n)]
        d = remote(view, view, s, s, sib)
        d.wait()

    eye = (iota((T, T), 0) == iota((T, T), 1)).astype(F32)
    rows8 = iota((8, H), 0)
    rows = jnp.where(
        rows8 == 0, al_ref[...], jnp.where(rows8 == 1, sk_ref[...], bi_ref[...])
    )
    eye32 = (iota((H, H), 0) == iota((H, H), 1)).astype(F32)
    cols = nt_hi(eye32, rows)
    rate = -jnp.exp(cols[:, 0:1])
    raw = dt_ref[...] + cols[:, 2:3]
    tail = jnp.exp(-jnp.abs(raw))
    step = jnp.maximum(raw, 0.0) + jnp.log1p(tail)
    sg_ref[...] = jnp.where(raw >= 0, 1.0, tail) / (1.0 + tail)
    ld = rate * step
    ld_ref[...] = ld
    step_ref[...] = step
    upper = (iota((T, T), 0) <= iota((T, T), 1)).astype(F32)
    c2 = nn_hi(ld, upper) * LOG2E
    for i in range(PAIRS):
        c2_ref[i, 0:2, :] = c2[2 * i : 2 * i + 2]
    c3 = jnp.concatenate(split3(nt_hi(eye, c2)), axis=1)
    s3 = jnp.concatenate(split3(nt_hi(eye, step)), axis=1)
    spread_k = (iota((96, KL), 0) % H == iota((96, KL), 1) % H).astype(BF16)
    c_feet = nn(c3, spread_k)
    dec_mine[...] = jnp.broadcast_to(c_feet[T - 1 : T, 0:128], (8, 128))
    eye_b = (iota((N, N), 0) == iota((N, N), 1)).astype(BF16)
    bb, cc = b_ref[...], c_ref[...]
    bt = nt(eye_b, bb).astype(BF16)
    ct = nt(eye_b, cc).astype(BF16)

    fhi, flo = split(jnp.concatenate([f_ref[...], jnp.zeros((4, HP), F32)], axis=0))
    f48[...] = jnp.concatenate([fhi, flo, fhi], axis=0)
    e96[...] = (iota((96, HP), 0) % H == iota((96, HP), 1) // PS).astype(BF16)
    sk8 = jnp.broadcast_to(sk_ref[...], (8, H))
    row_sk[...] = nn(jnp.concatenate(split3(sk8), axis=1), e96[...])

    def block(i):
        return pl.ds(pl.multiple_of(i * WB, WB), WB)

    @pl.loop(0, BLOCKS, unroll=4)
    def _(i):
        blk = block(i)
        e3 = e96[:, blk]
        cb, sb = nn(c3, e3), nn(s3, e3)
        cexp[:, blk] = cb
        sexp[:, blk] = sb
        z = sb * x_ref[:, blk].astype(F32)
        hi, lo = split(z)
        zhi[:, blk] = hi
        zlo[:, blk] = lo
        hi, lo = split(jnp.exp2(cb[T - 1 : T] - cb) * z)
        whi[:, blk] = hi
        wlo[:, blk] = lo
        local_f[:, blk] = nn(bt, hi) + nn(bt, lo)

    pl.semaphore_wait(barrier, chips + g2n)

    mine_half = pl.ds(pl.multiple_of(core * 64, 64), 64)
    sib_half = pl.ds(pl.multiple_of(64 - core * 64, 64), 64)
    ex_dec = remote(dec_mine, sib_dec, 5, 5, sib)
    ex = [
        remote(local_f.at[sib_half], sib_f.at[sib_half], 1, 1, sib),
        remote(local_r.at[sib_half], sib_r.at[sib_half], 2, 2, sib),
        remote(local_f.at[mine_half], sib_f.at[mine_half], 3, 3, sib),
        remote(local_r.at[mine_half], sib_r.at[mine_half], 4, 4, sib),
    ]
    ex_dec.start()
    ex[0].start()

    def reverse(i):
        blk = block(i)
        hi, lo = split(jnp.exp2(cexp[:, blk]) * og_ref[:, blk].astype(F32))
        local_r[:, blk] = nn(ct, hi) + nn(ct, lo)

    pl.loop(0, BLOCKS // 2, unroll=2)(reverse)
    ex_dec.wait()
    row_sib[...] = jnp.exp2(
        nn(jnp.concatenate(split3(sib_dec[:, 0:H]), axis=1), e96[...])
    )
    ex[0].wait()

    def part(o):
        return (
            pl.ds(pl.multiple_of(o // lbs * 8, 8), 8),
            pl.ds(pl.multiple_of(o % lbs * lanes, 128), lanes),
        )

    my_r, my_l = part(chip)

    @pl.loop(0, BLOCKS)
    def _(i):
        blk = block(i)
        d_sib = row_sib[0:1, blk]
        d_me = jnp.exp2(cexp[T - 8 : T, blk])[7:8]
        one = jnp.ones_like(d_me)
        half_f[:, blk] = (
            jnp.where(first, d_sib, one) * local_f[mine_half, blk]
            + jnp.where(first, one, d_me) * sib_f[mine_half, blk]
        )

    @pl.loop(1, chips)
    def _(k):
        o = lax.rem(chip + k, chips)
        r, l = part(o)
        remote(half_f.at[r, l], got_f.at[chip], 6, 6, o * 2 + core).start()

    got_f[chip] = half_f[my_r, my_l]
    dec_row[...] = dec_mine[0:1] + sib_dec[0:1]
    decs[chip] = dec_row[...]
    pl.loop(BLOCKS // 2, BLOCKS, unroll=2)(reverse)
    ex[1].start()
    ex[2].start()
    ex[3].start()

    @pl.loop(1, chips)
    def _(k):
        o = lax.rem(chip + k, chips)
        remote(dec_row, decs.at[chip], 0, 0, o * 2 + core).start()

    scores = nt(cc, bb)
    sc_ref[...] = jnp.where(iota((T, T), 0) >= iota((T, T), 1), scores, 0.0)
    scores = nt(bb, cc)
    sct_ref[...] = jnp.where(iota((T, T), 0) <= iota((T, T), 1), scores, 0.0)

    low_lanes = iota((128, 128), 1) < PS

    def inner(i):
        blk = pl.ds(pl.multiple_of(i * 128, 128), 128)
        rhs = jnp.concatenate([zhi[:, blk], zlo[:, blk]], axis=1)
        cb = cexp[:, blk]
        for r in range(2):
            seen = 128 * (r + 1)
            at = slice(128 * r, seen)
            outs = []
            for e in range(2):
                col = cb[at, PS * e : PS * e + 1]
                row = c2_ref[i, e : e + 1, 0:seen]
                mix = sc_ref[at, 0:seen] * jnp.exp2(jnp.minimum(col - row, 0.0))
                hi, lo = split(mix)
                res = nn(hi, rhs[0:seen]) + nn(lo, rhs[0:seen])
                outs.append(res[:, 0:128] + res[:, 128:256])
            yv[at, blk] = jnp.where(low_lanes, outs[0], outs[1])

    pl.loop(0, 3)(inner)
    ex[1].wait()

    @pl.loop(0, BLOCKS)
    def _(i):
        blk = block(i)
        d_sib = row_sib[0:1, blk]
        d_me = jnp.exp2(cexp[T - 8 : T, blk])[7:8]
        one = jnp.ones_like(d_me)
        half_r[:, blk] = (
            jnp.where(first, one, d_sib) * local_r[mine_half, blk]
            + jnp.where(first, d_me, one) * sib_r[mine_half, blk]
        )

    got_r[chip] = half_r[my_r, my_l]

    pl.loop(3, 9)(inner)
    arrived(decs, chips - 1, 0)
    dall = decs[:, 0, :]
    dec_all[...] = jnp.exp2(dall)
    head0 = chip % lbs * (lanes // PS)
    spread_l = (iota((128, lanes), 0) == head0 + iota((128, lanes), 1) // PS).astype(F32)
    chip_dec = jnp.exp2(nn_hi(dall, spread_l))

    arrived(got_f, chips - 1, 6)
    acc = jnp.zeros((8, lanes), F32)
    for q in range(chips):
        ret_f[q] = acc
        acc = got_f[q] + chip_dec[q : q + 1] * acc

    @pl.loop(1, chips)
    def _(k):
        o = lax.rem(chip + k, chips)
        r = pl.ds(pl.multiple_of(core * 64 + chip // lbs * 8, 8), 8)
        remote(ret_f.at[o], s_in.at[r, my_l], 8, 8, o * 2 + core).start()

    own = pl.ds(pl.multiple_of(core * 64 + chip // lbs * 8, 8), 8)
    s_in[own, my_l] = ret_f[chip]
    pl.loop(9, PAIRS)(inner)

    @pl.loop(0, BLOCKS)
    def _(i):
        blk = block(i)
        eh = e96[0:H, blk]
        fhi, flo = f48[0:16, blk], f48[16:32, blk]
        for k in range(FEET):
            rows_k = slice(k * H, k * H + H)
            bhi[rows_k, blk] = jnp.where(eh > 0, jnp.broadcast_to(fhi[k : k + 1], eh.shape), 0.0).astype(BF16)
            blo[rows_k, blk] = jnp.where(eh > 0, jnp.broadcast_to(flo[k : k + 1], eh.shape), 0.0).astype(BF16)

    ex[2].wait()
    ex[3].wait()
    arrived(ret_f, chips - 1, 8)
    back_f = remote(s_in.at[mine_half], s_in.at[mine_half], 10, 10, sib)
    back_f.start()

    @pl.loop(1, chips)
    def _(k):
        o = lax.rem(chip + k, chips)
        r, l = part(o)
        remote(half_r.at[r, l], got_r.at[chip], 7, 7, o * 2 + core).start()

    back_f.wait()

    vel[...] = jnp.zeros_like(vel)

    @pl.loop(0, BLOCKS, unroll=8)
    def _(i):
        blk = block(i)
        state = s_in[:, blk]
        state = jnp.where(first, state, sib_f[:, blk] + row_sib[0:1, blk] * state)
        s_in[:, blk] = state
        hi, lo = split(state)
        y = yv[:, blk] + jnp.exp2(cexp[:, blk]) * (nn(cc, hi) + nn(cc, lo))
        yv[:, blk] = y
        hi, lo = split(y + row_sk[0:1, blk] * x_ref[:, blk].astype(F32))
        both = nt(hi, f48[0:32, blk])
        vel[:, 0:16] += both[:, 0:16] + both[:, 16:32] + nt(lo, f48[0:16, blk])

    touch = jnp.broadcast_to(ct_ref[...].astype(F32), (8, T))
    touch = nt_hi(eye, touch)[:, 0:1]
    lane = iota((T, 128), 1)
    row = iota((T, 128), 0)
    v = jnp.where(lane == FEET, touch, vel[...])
    vel[...] = v
    to_next = remote(vel.at[pl.ds(T - 8, 8)], vel_prev, 12, 12, ring(1))
    to_prev = remote(vel.at[pl.ds(0, 8)], vel_next, 13, 13, ring(nf - 1))
    to_next.start()
    to_prev.start()
    to_next.wait()
    to_prev.wait()
    feet = lane < FEET
    before = jnp.where(row == 0, vel_prev[7:8, :], pltpu.roll(v, 1, 0))
    slide = jnp.where(
        feet & ((row > 0) | (me > 0)), touch * (v - before), 0.0
    )
    nxt = vel_next[0:1, :]
    edge = nxt[:, FEET : FEET + 1] * (nxt - v[T - 1 : T, :])
    edge = jnp.where((iota((1, 128), 1) < FEET) & (me < nf - 1), edge, 0.0)
    change = slide - jnp.where(row == T - 1, edge, pltpu.roll(slide, T - 1, 0))
    chi, clo = split(change)

    feet_of = (iota((128, KL), 0) == iota((128, KL), 1) // H).astype(BF16)
    hi, lo = split(jnp.exp2(c_feet) * (nn(chi, feet_of) + nn(clo, feet_of)))
    gd_local[...] = nn(ct, hi) + nn(ct, lo)

    gd_ex = remote(gd_local, gd_sib, 18, 18, sib)
    gd_ex.start()

    def tile(o, base):
        return (
            pl.ds(pl.multiple_of(base + o // 4 * 8, 8), 8),
            pl.ds(pl.multiple_of(o % 4 * 128, 128), 128),
        )

    c48 = jnp.concatenate([chi[:, 0:16], chi[:, 0:16], clo[:, 0:16]], axis=1)

    def total_grad(i):
        blk = block(i)
        hi, lo = split(og_ref[:, blk].astype(F32) + nn(c48, f48[:, blk]))
        dyhi[:, blk] = hi
        dylo[:, blk] = lo

    pl.loop(0, BLOCKS // 2, unroll=2)(total_grad)
    gd_ex.wait()
    decay_me = jnp.exp2(jnp.concatenate([dec_mine[0:1]] * 4, axis=1))
    decay_sib = jnp.exp2(jnp.concatenate([sib_dec[0:1]] * 4, axis=1))
    one = jnp.ones_like(decay_me)
    gd_half[...] = (
        jnp.where(first, one, decay_sib) * gd_local[mine_half, :]
        + jnp.where(first, decay_me, one) * gd_sib[mine_half, :]
    )

    @pl.loop(1, chips)
    def _(k):
        o = lax.rem(chip + k, chips)
        r, l = tile(o, 0)
        remote(gd_half.at[r, l], gd_got.at[chip], 14, 14, o * 2 + core).start()

    gd_r, gd_l = tile(chip, 0)
    gd_got[chip] = gd_half[gd_r, gd_l]
    gd_r, gd_l = tile(chip, core * 64)
    pl.loop(BLOCKS // 2, BLOCKS, unroll=2)(total_grad)
    arrived(got_r, chips - 1, 7)
    acc = jnp.zeros((8, lanes), F32)
    for q in reversed(range(chips)):
        ret_r[q] = acc
        acc = got_r[q] + chip_dec[q : q + 1] * acc

    @pl.loop(1, chips)
    def _(k):
        o = lax.rem(chip + k, chips)
        r = pl.ds(pl.multiple_of(core * 64 + chip // lbs * 8, 8), 8)
        remote(ret_r.at[o], g_end.at[r, my_l], 9, 9, o * 2 + core).start()

    g_end[own, my_l] = ret_r[chip]

    ds0[...] = jnp.zeros_like(ds0)
    ds1[...] = jnp.zeros_like(ds1)
    zero_b = jnp.zeros((128, 128), BF16)

    def backward(i):
        blk = pl.ds(pl.multiple_of(i * 128, 128), 128)
        dh, dl = dyhi[:, blk], dylo[:, blk]
        rhs = jnp.concatenate([dh, dl], axis=1)
        twice = jnp.concatenate([dh, dh], axis=1)
        cb = cexp[:, blk]
        for r, acc in ((0, ds0), (1, ds1)):
            at, on = slice(128 * r, 128 * r + 128), slice(128 * r, T)
            zh, zl = zhi[at, blk], zlo[at, blk]
            outs = []
            total = acc[...]
            for e in range(2):
                keep = low_lanes if e == 0 else ~low_lanes
                zhe = jnp.where(keep, zh, zero_b)
                zle = jnp.where(keep, zl, zero_b)
                col = cb[at, PS * e : PS * e + 1]
                fall = jnp.exp2(jnp.minimum(c2_ref[i, e : e + 1, on] - col, 0.0))
                w = nt(jnp.concatenate([zhe, zle], axis=1), twice[on]) + nt(zhe, dl[on])
                total = total + fall * w
                hi, lo = split(sct_ref[at, on] * fall)
                res = nn(hi, rhs[on]) + nn(lo, rhs[on])
                outs.append(res[:, 0:128] + res[:, 128:256])
            acc[...] = total
            dz[at, blk] = jnp.where(low_lanes, outs[0], outs[1])

    pl.loop(0, 5)(backward)

    arrived(gd_got, chips - 1, 14)
    acc = jnp.zeros((8, 128), F32)
    for q in reversed(range(chips)):
        gd_ret[q] = acc
        acc = gd_got[q] + dec_all[q : q + 1] * acc

    @pl.loop(1, chips)
    def _(k):
        o = lax.rem(chip + k, chips)
        remote(gd_ret.at[o], gd_end.at[gd_r, gd_l], 15, 15, o * 2 + core).start()

    gd_end[gd_r, gd_l] = gd_ret[chip]
    pl.loop(5, PAIRS)(backward)

    m0 = iota((128, T), 0) <= iota((128, T), 1)
    m1 = iota((128, 128), 0) <= iota((128, 128), 1)
    dst = jnp.concatenate(
        [
            jnp.where(m0, ds0[...], 0.0),
            jnp.concatenate(
                [jnp.zeros((128, 128), F32), jnp.where(m1, ds1[...], 0.0)], axis=1
            ),
        ],
        axis=0,
    )
    hi, lo = split(dst)
    gb_ref[...] = nn(hi, cc) + nn(lo, cc)
    p1[...] = jnp.zeros_like(p1)
    eye_t = eye.astype(BF16)
    hi = nt(eye_t, hi).astype(BF16)
    lo = nt(eye_t, lo).astype(BF16)
    gc_ref[...] = nn(hi, bb) + nn(lo, bb)

    @pl.loop(0, BLOCKS, unroll=2)
    def _(i):
        blk = block(i)
        dy = dyhi[:, blk].astype(F32) + dylo[:, blk].astype(F32)
        hi, lo = split(jnp.exp2(cexp[:, blk]) * dy)
        shi, slo = split(s_in[:, blk])
        gc_ref[...] += nt(hi, shi) + nt(lo, shi) + nt(hi, slo)
        x = x_ref[:, blk].astype(F32)
        hi, lo = split(yv[:, blk] * dy)
        eh = e96[0:H, blk]
        p1[...] += nt(eh, hi) + nt(eh, lo)
        row_d[:, blk] = jnp.broadcast_to(jnp.sum(x * dy, axis=0, keepdims=True), (8, WB))

    arrived(ret_r, chips - 1, 9)
    back_r = remote(g_end.at[mine_half], g_end.at[mine_half], 11, 11, sib)
    back_r.start()
    arrived(gd_ret, chips - 1, 15)
    gd_back = remote(gd_end.at[mine_half], gd_end.at[mine_half], 19, 19, sib)
    gd_back.start()
    gd_back.wait()
    back_r.wait()

    p2[...] = jnp.zeros_like(p2)
    gd_all = gd_end[...]
    gd_all = jnp.where(first, gd_sib[...] + decay_sib * gd_all, gd_all)
    gdh, gdl = split(gd_all[:, 0 : FEET * H])

    @pl.loop(0, BLOCKS, unroll=4)
    def _(i):
        blk = block(i)
        eh = e96[0:H, blk]
        grad = g_end[:, blk]
        grad = jnp.where(first, sib_r[:, blk] + row_sib[0:1, blk] * grad, grad)
        grad = grad + nn(gdh, bhi[:, blk]) + nn(gdl, bhi[:, blk]) + nn(gdh, blo[:, blk])
        g_end[:, blk] = grad
        ghi, glo = split(grad)
        cb = cexp[:, blk]
        last = cb[T - 1 : T]
        dzb = dz[:, blk] + jnp.exp2(last - cb) * (nn(bb, ghi) + nn(bb, glo))
        dz[:, blk] = dzb
        xdz = x_ref[:, blk].astype(F32) * dzb
        hi, lo = split(xdz)
        p2[...] += nt(eh, hi) + nt(eh, lo)
        s_last = jnp.exp2(last) * s_in[:, blk] + local_f[:, blk]
        row_b[:, blk] = jnp.broadcast_to(jnp.sum(grad * s_last, axis=0, keepdims=True), (8, WB))

    heads = (iota((H, HP), 0) == iota((H, HP), 1) // PS).astype(F32)
    edge_h = nt_hi(heads, row_b[...])[:, 0:1]
    skip_h = nt_hi(row_d[...], heads)
    later = (iota((T, T), 0) >= iota((T, T), 1)).astype(F32)
    dld = nn_hi(p1[...] - step_ref[...] * p2[...], later) + edge_h
    gdt = (rate * dld + p2[...]) * sg_ref[...]
    gdt_ref[...] = gdt
    ones8 = jnp.ones((8, T), F32)
    log_h = nt_hi(ones8, dld * ld_ref[...])
    bias_h = nt_hi(ones8, gdt)
    hsum[...] = jnp.zeros_like(hsum)
    hsum[:, 0:H] = jnp.where(rows8 == 0, log_h, jnp.where(rows8 == 1, skip_h, bias_h))

    @pl.loop(1, G1)
    def _(k):
        j = lax.rem(low + k, G1)
        remote(hsum, hgot1.at[low], 16, 16, (group * G1 + j) * 2 + core).start()

    hgot1[low] = hsum[...]

    def sources(i):
        blk = block(i)
        dy = dyhi[:, blk].astype(F32) + dylo[:, blk].astype(F32)
        gx_ref[:, blk] = (row_sk[0:1, blk] * dy + sexp[:, blk] * dz[:, blk]).astype(BF16)
        hi, lo = whi[:, blk], wlo[:, blk]
        ghi, glo = split(g_end[:, blk])
        gb_ref[...] += nt(hi, ghi) + nt(lo, ghi) + nt(hi, glo)

    pl.loop(0, BLOCKS // 2, unroll=4)(sources)
    arrived(hgot1, G1 - 1, 16)
    hmid[...] = jnp.sum(hgot1[...], axis=0)

    @pl.loop(1, g2n)
    def _(k):
        frame, dp = second(k)
        remote(hmid, hgot2.at[spot], 17, 17, frame, dp).start()

    hgot2[spot] = hmid[...]
    pl.loop(BLOCKS // 2, BLOCKS, unroll=4)(sources)
    arrived(hgot2, g2n - 1, 17)
    hg_ref[...] = jnp.sum(hgot2[...], axis=0)


def hand_out(gx, gb, gc, gdt, hg, gx_o, gb_o, gc_o, gdt_o, hg_o, sem):
    pairs = ((gx, gx_o), (gb, gb_o), (gc, gc_o), (gdt, gdt_o))
    copies = [
        pltpu.make_async_copy(a, b.at[0], sem.at[k]) for k, (a, b) in enumerate(pairs)
    ]
    for copy in copies:
        copy.start()
    hg_o[...] = hg[0:3, 0:H]
    for copy in copies:
        copy.wait()


def on_device(dp_n, nf, layer_in, in_b, in_c, dt_raw, a_log, skip_gain, dt_bias, foot_map, contact, out_grad):
    chips = nf // 2
    lanes = HP // (chips // 8)
    vm = lambda *shape: pltpu.VMEM(shape, F32)
    vb = lambda *shape: pltpu.VMEM(shape, BF16)
    whole = pl.BlockSpec(memory_space=pltpu.VMEM)
    gx, gb, gc, gdt, hg = pl.pallas_call(
        functools.partial(kernel, dp_n, nf),
        out_shape=(
            jax.ShapeDtypeStruct((T, HP), BF16),
            jax.ShapeDtypeStruct((T, N), F32),
            jax.ShapeDtypeStruct((T, N), F32),
            jax.ShapeDtypeStruct((H, T), F32),
            jax.ShapeDtypeStruct((8, 128), F32),
        ),
        in_specs=[whole] * 10,
        out_specs=[whole] * 5,
        scratch_shapes=[
            vm(N, HP),
            vm(N, HP),
            vm(N, HP),
            vm(N, HP),
            vm(N // 2, HP),
            vm(N // 2, HP),
            vm(chips, 8, lanes),
            vm(chips, 8, lanes),
            vm(chips, 8, lanes),
            vm(chips, 8, lanes),
            vm(N, HP),
            vm(N, HP),
            vm(T, HP),
            vm(T, HP),
            vm(T, HP),
            vm(T, HP),
            vb(T, HP),
            vb(T, HP),
            vb(T, HP),
            vb(T, HP),
            vb(T, HP),
            vb(T, HP),
            vb(FEET * H, HP),
            vb(FEET * H, HP),
            vb(48, HP),
            vb(96, HP),
            vm(8, HP),
            vm(8, HP),
            vm(PAIRS, 8, T),
            vm(H, T),
            vm(H, T),
            vm(H, T),
            vm(T, T),
            vm(T, T),
            vm(128, T),
            vm(128, 128),
            vm(8, 128),
            vm(1, 128),
            vm(chips, 1, 128),
            vm(8, 128),
            vm(chips, 128),
            vm(T, 128),
            vm(8, 128),
            vm(8, 128),
            vm(N, KL),
            vm(N, KL),
            vm(N // 2, KL),
            vm(chips, 8, 128),
            vm(chips, 8, 128),
            vm(N, KL),
            vm(H, T),
            vm(H, T),
            vm(8, HP),
            vm(8, HP),
            vm(8, 128),
            vm(G1, 8, 128),
            vm(8, 128),
            vm(dp_n * (nf // G1), 8, 128),
            pltpu.SemaphoreType.DMA((20,)),
            pltpu.SemaphoreType.DMA((20,)),
        ],
        compiler_params=pltpu.CompilerParams(
            collective_id=0, has_side_effects=True, vmem_limit_bytes=56 * 2**20
        ),
    )(
        layer_in[0],
        in_b[0],
        in_c[0],
        dt_raw[0],
        a_log[None],
        skip_gain[None],
        dt_bias[None],
        foot_map,
        contact,
        out_grad[0],
    )
    place = pl.BlockSpec(memory_space=pl.ANY)
    return pl.pallas_call(
        hand_out,
        out_shape=(
            jax.ShapeDtypeStruct((1, T, HP), BF16),
            jax.ShapeDtypeStruct((1, T, N), F32),
            jax.ShapeDtypeStruct((1, T, N), F32),
            jax.ShapeDtypeStruct((1, H, T), F32),
            jax.ShapeDtypeStruct((3, H), F32),
        ),
        in_specs=[whole] * 5,
        out_specs=[place] * 4 + [whole],
        scratch_shapes=[pltpu.SemaphoreType.DMA((4,))],
    )(gx, gb, gc, gdt, hg)


def solution(mesh):
    return jax.shard_map(
        functools.partial(on_device, mesh.shape["dp"], mesh.shape["frame"]),
        mesh=mesh,
        in_specs=(
            P("dp", "frame", None),
            P("dp", "frame", None),
            P("dp", "frame", None),
            P("dp", None, "frame"),
            P(),
            P(),
            P(),
            P(),
            P("dp", "frame"),
            P("dp", "frame", None),
        ),
        out_specs=(
            P("dp", "frame", None),
            P("dp", "frame", None),
            P("dp", "frame", None),
            P("dp", None, "frame"),
            P(),
        ),
        check_vma=False,
    )
```
